256 devices in a mesh: blk: 64 (over y, z, x_lo), hid: 4 (over x_hi, core).
Axes of the slice: x: 4 (x_hi: 2, x_lo: 2; x = x_hi * 2 + x_lo), y: 4, z: 8, core: 2. Of those that a mesh axis runs over, the one named last changes fastest.
Arguments:
- gate_pre: bfloat16 [20480, 7168], P('blk', 'hid'), may hold values from -8 to 8
- up_pre: bfloat16 [20480, 7168], P('blk', 'hid'), may hold values from -6 to 6
- down_weight: bfloat16 [2560, 7168], P('blk', 'hid'), may hold values from -0.0625 to 0.0625
- cotangent: bfloat16 [20480, 2560], P('blk', 'hid'), may hold values from -16 to 16
Outputs:
- mixed: bfloat16 [20480, 2560], P('blk', 'hid')
- grad_gate: bfloat16 [20480, 7168], P('blk', 'hid')
- grad_up: bfloat16 [20480, 7168], P('blk', 'hid')
- weight_grad: float32 [2560, 7168], P('blk', 'hid')
The draws below stay inside these ranges and needn't reach their ends.
All inputs are finite; a program needn't handle non-finite values.
Results may differ from the reference program's by a relative error of at most 0.0049.
Values may be sent and summed in bfloat16 or wider, within the bound.
No kernel may reach another device: no remote copies, remote signals or barrier semaphores. Data moves between devices by JAX's collectives and lax.ppermute only.
A program may use at most 384 MiB of HBM per device.

```python
import jax
import jax.numpy as jnp

D = 2560
FF = 7168
TOKENS = 20480


def spiked(drawn, stream_key, source, target, blocks, factor):
    owner, partner = [(jnp.arange(drawn.shape[position]) // (drawn.shape[position] // blocks)).reshape([-1 if axis == position else 1 for axis in range(drawn.ndim)]) for position in (source, target)]
    chosen = jax.random.permutation(stream_key, blocks)[partner]
    strong = (owner == chosen) | (owner == (partner + blocks // 2) % blocks)
    return jnp.where(strong, factor * drawn, drawn)


def block_levels(key, shape, shards, least, high):
    def one(dim, shards_of):
        draws = jax.random.uniform(jax.random.fold_in(jax.random.fold_in(key, 6), dim), (shards_of,), jnp.float32, least / len(shards), high / len(shards))
        return jnp.repeat(jnp.exp(draws), shape[dim] // shards_of).reshape((-1,) + (1,) * (len(shape) - dim - 1))

    factor_of = one(*shards[0])
    for cut in shards[1:]:
        factor_of = factor_of * one(*cut)
    return factor_of


def bell_draw(own_key, dims, scale, reach, split=(), kind=jnp.bfloat16):
    entries = scale * jax.random.normal(own_key, dims, jnp.float32)
    if split:
        entries = entries * block_levels(own_key, dims, split, -0.22, 0.18)
    return jnp.clip(entries, -reach, reach).astype(kind)


def noise_with(rng, shape, scale, limit, cuts, heavy, kind=jnp.bfloat16):
    result = scale * jax.random.normal(rng, shape, jnp.float32)
    if cuts:
        result = result * block_levels(rng, shape, cuts, -0.22, 0.18)
    return jnp.clip(spiked(result, jax.random.fold_in(rng, 3), *heavy), -limit, limit).astype(kind)


def setup_inputs(seed: int = 0) -> dict:
    splits = jax.random.split(jax.random.key(seed), 5)
    return {
        "gate_pre": bell_draw(splits[0], (TOKENS, FF), 1.5, 8.0, ((0, 64), (1, 4))),
        "up_pre": bell_draw(splits[1], (TOKENS, FF), 1.0, 6.0, ((0, 64), (1, 4))),
        "down_weight": bell_draw(splits[2], (D, FF), FF ** -0.5, 0.0625, ((0, 64), (1, 4))),
        "cotangent": noise_with(splits[3], (TOKENS, D), 1.0, 16.0, ((0, 64), (1, 4)), (0, 1, 64, 4.0)),
    }


def reference(gate_pre, up_pre, down_weight, cotangent):
    gate_value = gate_pre.astype(jnp.float32)
    up_value = up_pre.astype(jnp.float32)
    sigmoid_gate = jax.nn.sigmoid(gate_value)
    activated = gate_value * sigmoid_gate
    hidden = (activated * up_value).astype(jnp.bfloat16)
    mixed = jnp.dot(hidden, down_weight.T, preferred_element_type=jnp.float32).astype(jnp.bfloat16)
    grad_hidden = jnp.dot(cotangent, down_weight, preferred_element_type=jnp.float32)
    grad_gate = (grad_hidden * up_value * sigmoid_gate * (1.0 + gate_value * (1.0 - sigmoid_gate))).astype(jnp.bfloat16)
    grad_up = (grad_hidden * activated).astype(jnp.bfloat16)
    weight_grad = jnp.dot(cotangent.T, hidden, preferred_element_type=jnp.float32)
    return mixed, grad_gate, grad_up, weight_grad
```

```python
import jax
import jax.numpy as jnp
import numpy as np
from jax import lax
from jax.sharding import Mesh, PartitionSpec as P

SIZES = {"y": 4, "z": 8, "xl": 2, "xh": 2, "c": 2}
CUTS = ((0, 896), (896, 1792))


def shift(value, axis, step):
    n = SIZES[axis]
    return lax.ppermute(value, axis, [(i, (i + step) % n) for i in range(n)])


def shift_x(value, step):
    def place(x):
        return (x % 2) * 2 + x // 2

    return lax.ppermute(value, ("xl", "xh"), [(place(x), place((x + step) % 4)) for x in range(4)])


def regroup():
    order = np.arange(640).reshape(8, 2, 40).transpose(1, 0, 2).reshape(-1)
    return np.eye(640, dtype=np.float32)[order].astype(jnp.bfloat16)


def dot(a, b, ca, cb, kind=jnp.float32):
    return lax.dot_general(a, b, (((ca,), (cb,)), ((), ())), preferred_element_type=jnp.float32).astype(kind)


def pick(flag, a, b):
    return jnp.where(flag, a, b)


def shards(gate_pre, up_pre, down_weight, cotangent):
    bf16 = jnp.bfloat16
    iy, iz, ixl, ixh, ic = (lax.axis_index(a) for a in ("y", "z", "xl", "xh", "c"))
    low, first, core0 = ixl == 0, ixh == 0, ic == 0
    gate_value = gate_pre.astype(jnp.float32)
    up_value = up_pre.astype(jnp.float32)
    sigmoid_gate = jax.nn.sigmoid(gate_value)
    activated = gate_value * sigmoid_gate
    hidden = (activated * up_value).astype(bf16)
    order = jnp.asarray(regroup())

    weights = [lax.all_gather(down_weight[:, a:b], ("y", "z"), axis=0, tiled=True) for a, b in CUTS]

    turned = dot(order, cotangent, 1, 1, bf16).reshape(2, 320, 320)
    own_part = lax.dynamic_index_in_dim(turned, ixl, 0, False)
    other_part = lax.dynamic_index_in_dim(turned, 1 - ixl, 0, False)
    from_left = shift_x(other_part, 1)
    from_right = shift_x(other_part, -1)
    from_far = shift_x(own_part, 2)
    mine = jnp.stack([own_part, from_far, pick(low, from_right, from_left), pick(low, from_left, from_right)])
    theirs = shift(mine, "c", 1)

    def whole(same, other):
        here = [pick(core0, mine[same], theirs[same]), pick(core0, theirs[same], mine[same])]
        there = [pick(core0, mine[other], theirs[other]), pick(core0, theirs[other], mine[other])]
        blocks = [pick(first, here[0], there[0]), pick(first, here[1], there[1])]
        blocks += [pick(first, there[0], here[0]), pick(first, there[1], here[1])]
        return jnp.concatenate(blocks, axis=0)

    cot_own, cot_pair = whole(0, 1), whole(2, 3)
    own_hidden = [hidden[:, a:b] for a, b in CUTS]
    pair_hidden = [shift(h, "xl", 1) for h in own_hidden]

    cot_own4, cot_pair4 = cot_own.reshape(4, 8, 40, 320), cot_pair.reshape(4, 8, 40, 320)

    def block(z, q):
        rows = [lax.dynamic_index_in_dim(t, z % 8, 1, False).reshape(160, 320) for t in (cot_own4, cot_pair4)]
        return dot(rows[0], own_hidden[q], 1, 0) + dot(rows[1], pair_hidden[q], 1, 0)

    sums = []
    for q in range(2):
        running = {}
        for way, hops in ((1, 4 - q), (-1, 3 + q)):
            value = block(iz + way * hops, q)
            for left in range(hops - 1, -1, -1):
                got = shift(value.astype(bf16), "z", way)
                value = got.astype(jnp.float32)
                if left:
                    value = value + block(iz + way * left, q)
            running[way] = value
        sums.append((running[1] + running[-1] + block(iz, q)).reshape(4, 40, 896))
    summed = jnp.concatenate(sums, axis=2)
    weight_grad = lax.dynamic_index_in_dim(summed, iy, 0, False)
    for step in (1, 2, 3):
        part = lax.dynamic_index_in_dim(summed, (iy + step) % 4, 0, False).astype(bf16)
        weight_grad = weight_grad + shift(part, "y", step).astype(jnp.float32)

    grads = []
    for q in range(2):
        sent = shift(dot(cot_pair, weights[q], 0, 0, bf16), "xl", 1)
        grads.append(dot(cot_own, weights[q], 0, 0) + sent.astype(jnp.float32))
    grad_hidden = jnp.concatenate(grads, axis=1)
    grad_gate = (
        grad_hidden * up_value * sigmoid_gate * (1.0 + gate_value * (1.0 - sigmoid_gate))
    ).astype(bf16)
    grad_up = (grad_hidden * activated).astype(bf16)

    def partial(h):
        return sum(dot(weights[q], h[q], 1, 1) for q in range(2)).reshape(2, 2, 320, 320)

    out_own, out_pair = partial(own_hidden), partial(pair_hidden)
    both = jnp.stack([out_own, out_pair])
    keep = lax.dynamic_index_in_dim(both, ic, 2, False)
    give = lax.dynamic_index_in_dim(both, 1 - ic, 2, False).astype(bf16)
    added = keep + shift(give, "c", 1).astype(jnp.float32)
    near = lax.dynamic_index_in_dim(added, ixh, 1, False)
    far = lax.dynamic_index_in_dim(added, 1 - ixh, 1, False).astype(bf16)
    near_pair = near[1].astype(bf16)
    left = shift_x(pick(low, near_pair, far[1]), 1)
    right = shift_x(pick(low, far[1], near_pair), -1)
    across = shift_x(far[0], 2)
    own_rows = (near[0] + across.astype(jnp.float32)).astype(bf16)
    other_rows = (left.astype(jnp.float32) + right.astype(jnp.float32)).astype(bf16)
    rows = jnp.concatenate([pick(low, own_rows, other_rows), pick(low, other_rows, own_rows)], axis=0)
    mixed = dot(rows, order, 0, 0, bf16)
    return (mixed, grad_gate, grad_up, weight_grad)


def solution(mesh):
    fine = Mesh(mesh.devices.reshape(4, 8, 2, 2, 2), ("y", "z", "xl", "xh", "c"))
    placed = P(("y", "z", "xl"), ("xh", "c"))
    return jax.shard_map(
        shards,
        mesh=fine,
        in_specs=(placed,) * 4,
        out_specs=(placed,) * 4,
        check_vma=False,
    )
```

```python
import jax
import jax.numpy as jnp
import numpy as np
from jax import lax
from jax.experimental import pallas as pl
from jax.experimental.pallas import tpu as pltpu
from jax.sharding import Mesh, PartitionSpec as P

SIZES = {"y": 4, "z": 8, "xl": 2, "xh": 2, "c": 2}
CUTS = ((0, 896), (896, 1792))


def shift(value, axis, step):
    n = SIZES[axis]
    return lax.ppermute(value, axis, [(i, (i + step) % n) for i in range(n)])


def shift_x(value, step):
    def place(x):
        return (x % 2) * 2 + x // 2

    return lax.ppermute(value, ("xl", "xh"), [(place(x), place((x + step) % 4)) for x in range(4)])


def regroup():
    order = np.arange(640).reshape(8, 2, 40).transpose(1, 0, 2).reshape(-1)
    return np.eye(640, dtype=np.float32)[order].astype(jnp.bfloat16)


def dot(a, b, ca, cb, kind=jnp.float32):
    return lax.dot_general(a, b, (((ca,), (cb,)), ((), ())), preferred_element_type=jnp.float32).astype(kind)


def pick(flag, a, b):
    return jnp.where(flag, a, b)


def sync(*values):
    return lax.optimization_barrier(values)


def turn_kernel(which, order, cotangent, own, other):
    i = which[0]
    for place, part in ((i, own), (1 - i, other)):
        part[...] = dot(order[place], cotangent[...], 1, 1, part.dtype)


def turn(which, order, cotangent):
    vmem = pl.BlockSpec(memory_space=pltpu.VMEM)
    return pl.pallas_call(
        turn_kernel,
        out_shape=[jax.ShapeDtypeStruct((320, 320), jnp.bfloat16)] * 2,
        in_specs=[pl.BlockSpec(memory_space=pltpu.SMEM), vmem, vmem],
        out_specs=[vmem, vmem],
        cost_estimate=pl.CostEstimate(flops=2 * 640 * 640 * 320, bytes_accessed=1_700_000, transcendentals=0),
    )(which.reshape(1).astype(jnp.int32), order.reshape(2, 320, 640), cotangent)


def shards(gate_pre, up_pre, down_weight, cotangent):
    bf16 = jnp.bfloat16
    iy, iz, ixl, ixh, ic = (lax.axis_index(a) for a in ("y", "z", "xl", "xh", "c"))
    low, first, core0 = ixl == 0, ixh == 0, ic == 0
    gate_value = gate_pre.astype(jnp.float32)
    up_value = up_pre.astype(jnp.float32)
    sigmoid_gate = jax.nn.sigmoid(gate_value)
    activated = gate_value * sigmoid_gate
    hidden = (activated * up_value).astype(bf16)
    order = jnp.asarray(regroup())

    own_hidden = [hidden[:, a:b] for a, b in CUTS]

    own_part, other_part = turn(ixl, order, cotangent)
    rows = [down_weight] + [shift(down_weight, "y", -step) for step in (1, 2, 3)]
    pair_hidden = [shift(own_hidden[0], "xl", 1), None]
    rows, own_part, other_part, own_hidden[1] = sync(rows, own_part, other_part, own_hidden[1])

    held = jnp.stack(rows + rows[:3])
    held = lax.dynamic_slice_in_dim(held, (4 - iy) % 4, 4, 0)
    weight = lax.all_gather(held, "z", axis=1, tiled=True).reshape(1280, 1792)
    from_left = shift_x(other_part, 1)
    from_right = shift_x(other_part, -1)
    from_far = shift_x(own_part, 2)
    from_left, from_right, from_far, own_hidden[1] = sync(from_left, from_right, from_far, own_hidden[1])
    pair_hidden[1] = shift(own_hidden[1], "xl", 1)
    mine = jnp.stack([own_part, from_far, pick(low, from_right, from_left), pick(low, from_left, from_right)])
    theirs = shift(mine, "c", 1)
    theirs, pair_hidden[0] = sync(theirs, pair_hidden[0])

    def whole(same, other):
        here = [pick(core0, mine[same], theirs[same]), pick(core0, theirs[same], mine[same])]
        there = [pick(core0, mine[other], theirs[other]), pick(core0, theirs[other], mine[other])]
        blocks = [pick(first, here[0], there[0]), pick(first, here[1], there[1])]
        blocks += [pick(first, there[0], here[0]), pick(first, there[1], here[1])]
        return jnp.concatenate(blocks, axis=0)

    cot_own, cot_pair = whole(0, 1), whole(2, 3)

    cot_own4, cot_pair4 = cot_own.reshape(4, 320, 320), cot_pair.reshape(4, 320, 320)

    def block(step, q):
        pair = [lax.dynamic_index_in_dim(t, (iy + step) % 4, 0, False) for t in (cot_own4, cot_pair4)]
        return dot(pair[0], own_hidden[q], 1, 0) + dot(pair[1], pair_hidden[q], 1, 0)

    def wide(value):
        return value.astype(jnp.float32)

    up_two = shift(block(2, 0).astype(bf16), "y", 1)
    down_one = shift(block(-1, 0).astype(bf16), "y", -1)
    up_last = shift(block(1, 1).astype(bf16), "y", 1)
    down_two = shift(block(2, 1).astype(bf16), "y", -1)
    up_two, down_one, up_last, down_two = sync(up_two, down_one, up_last, down_two)
    up_one = shift((block(1, 0) + wide(up_two)).astype(bf16), "y", 1)
    down_last = shift((block(-1, 1) + wide(down_two)).astype(bf16), "y", -1)
    summed0 = block(0, 0) + wide(down_one)
    summed1 = block(0, 1) + wide(up_last)

    weights = [weight[:, a:b] for a, b in CUTS]
    shares = [dot(cot_pair, w, 0, 0, bf16) for w in weights]
    up_one, down_last, shares, summed0, summed1 = sync(up_one, down_last, shares, summed0, summed1)
    shares = [shift(share, "xl", 1) for share in shares]
    summed = jnp.concatenate([summed0 + wide(up_one), summed1 + wide(down_last)], axis=1).reshape(8, 40, 1792)

    def part(step):
        return lax.dynamic_index_in_dim(summed, (iz + step) % 8, 0, False)

    ring = {1: part(4), -1: part(-3)}

    def hop(hops):
        got = {1: shift(ring[1].astype(bf16), "z", 1)}
        if hops > 1:
            got[-1] = shift(ring[-1].astype(bf16), "z", -1)
        return got

    def add(got, hops):
        for way, left in ((1, hops), (-1, hops - 1)):
            if left > 1:
                ring[way] = wide(got[way]) + part(way * (left - 1))
            elif left:
                ring[way] = wide(got[way])

    got = sync(hop(4))[0]
    add(got, 4)
    got = hop(3)

    def partial(h, y):
        rows = weight[y * 320 : (y + 1) * 320]
        return dot(h, rows, 1, 1)

    hidden_pair = jnp.concatenate(pair_hidden, axis=1)
    parts = [[partial(h, y) for y in range(4)] for h in (hidden, hidden_pair)]
    give = jnp.stack([pick(core0, p[2 * k + 1], p[2 * k]).astype(bf16) for p in parts for k in range(2)])
    keep = [[pick(core0, p[2 * k], p[2 * k + 1]) for k in range(2)] for p in parts]
    got, give, shares[0] = sync(got, give, shares[0])
    add(got, 3)
    taken = shift(give, "c", 1)
    got = hop(2)
    got, taken = sync(got, taken)
    add(got, 2)
    got = hop(1)
    own = [dot(cot_own, w, 0, 0) for w in weights]
    got, own = sync(got, own)
    add(got, 1)
    weight_grad = part(0) + ring[1] + ring[-1]
    added = [[keep[t][k] + wide(taken[2 * t + k]) for k in range(2)] for t in range(2)]
    near = [pick(first, a[0], a[1]) for a in added]
    far = [pick(first, a[1], a[0]).astype(bf16) for a in added]
    near_pair = near[1].astype(bf16)
    left = shift_x(pick(low, near_pair, far[1]), 1)
    right = shift_x(pick(low, far[1], near_pair), -1)
    across = shift_x(far[0], 2)

    grad_hidden = jnp.concatenate([o + wide(s) for o, s in zip(own, shares)], axis=1)
    grad_gate = (
        grad_hidden * up_value * sigmoid_gate * (1.0 + gate_value * (1.0 - sigmoid_gate))
    ).astype(bf16)
    grad_up = (grad_hidden * activated).astype(bf16)
    own_cols = (near[0] + wide(across)).astype(bf16)
    other_cols = (wide(left) + wide(right)).astype(bf16)
    low_cols, high_cols = pick(low, own_cols, other_cols), pick(low, other_cols, own_cols)
    mixed = (dot(low_cols, order[:320], 1, 0) + dot(high_cols, order[320:], 1, 0)).astype(bf16)
    return (mixed, grad_gate, grad_up, weight_grad)


def solution(mesh):
    fine = Mesh(mesh.devices.reshape(4, 8, 2, 2, 2), ("y", "z", "xl", "xh", "c"))
    placed = P(("y", "z", "xl"), ("xh", "c"))
    return jax.shard_map(
        shards,
        mesh=fine,
        in_specs=(placed,) * 4,
        out_specs=(placed,) * 4,
        check_vma=False,
    )
```

```python
import jax
import jax.numpy as jnp
import numpy as np
from jax import lax
from jax.experimental import pallas as pl
from jax.experimental.pallas import tpu as pltpu
from jax.sharding import Mesh, PartitionSpec as P

SIZES = {"y": 4, "z": 8, "xl": 2, "xh": 2, "c": 2}
CUTS = ((0, 896), (896, 1792))


def shift(value, axis, step):
    n = SIZES[axis]
    return lax.ppermute(value, axis, [(i, (i + step) % n) for i in range(n)])


def shift_x(value, step):
    def place(x):
        return (x % 2) * 2 + x // 2

    return lax.ppermute(value, ("xl", "xh"), [(place(x), place((x + step) % 4)) for x in range(4)])


def regroup():
    order = np.arange(640).reshape(8, 2, 40).transpose(1, 0, 2).reshape(-1)
    return np.eye(640, dtype=np.float32)[order].astype(jnp.bfloat16)


def dot(a, b, ca, cb, kind=jnp.float32):
    return lax.dot_general(a, b, (((ca,), (cb,)), ((), ())), preferred_element_type=jnp.float32).astype(kind)


def pick(flag, a, b):
    return jnp.where(flag, a, b)


def sync(*values):
    return lax.optimization_barrier(values)


def turn_kernel(which, order, cotangent, own, other):
    i = which[0]
    for place, part in ((i, own), (1 - i, other)):
        part[...] = dot(order[place], cotangent[...], 1, 1, part.dtype)


def turn(which, order, cotangent):
    vmem = pl.BlockSpec(memory_space=pltpu.VMEM)
    return pl.pallas_call(
        turn_kernel,
        out_shape=[jax.ShapeDtypeStruct((320, 320), jnp.bfloat16)] * 2,
        in_specs=[pl.BlockSpec(memory_space=pltpu.SMEM), vmem, vmem],
        out_specs=[vmem, vmem],
        cost_estimate=pl.CostEstimate(flops=2 * 640 * 640 * 320, bytes_accessed=1_700_000, transcendentals=0),
    )(which.reshape(1).astype(jnp.int32), order.reshape(2, 320, 640), cotangent)


def output_kernel(which, own, pair0, pair1, weight, give, keep):
    core = which[0]
    for k in range(2):
        for slice_of, out in ((1 - core, give), (core, keep)):
            rows = pl.ds(pl.multiple_of((2 * k + slice_of) * 320, 320), 320)
            out[k] = dot(own[...], weight[rows, :], 1, 1, out.dtype)
            half = CUTS[0][1]
            value = dot(pair0[...], weight[rows, :half], 1, 1) + dot(pair1[...], weight[rows, half:], 1, 1)
            out[2 + k] = value.astype(out.dtype)


def output_parts(which, own, pair, weight):
    vmem = pl.BlockSpec(memory_space=pltpu.VMEM)
    return pl.pallas_call(
        output_kernel,
        out_shape=[jax.ShapeDtypeStruct((4, 320, 320), kind) for kind in (jnp.bfloat16, jnp.float32)],
        in_specs=[pl.BlockSpec(memory_space=pltpu.SMEM), vmem, vmem, vmem, vmem],
        out_specs=[vmem, vmem],
        compiler_params=pltpu.CompilerParams(vmem_limit_bytes=40 * 2**20),
        cost_estimate=pl.CostEstimate(flops=0, bytes_accessed=0, transcendentals=0),
    )(which.reshape(1).astype(jnp.int32), own, *pair, weight)


def shards(gate_pre, up_pre, down_weight, cotangent):
    bf16 = jnp.bfloat16
    iy, iz, ixl, ixh, ic = (lax.axis_index(a) for a in ("y", "z", "xl", "xh", "c"))
    low, first, core0 = ixl == 0, ixh == 0, ic == 0
    gate_value = gate_pre.astype(jnp.float32)
    up_value = up_pre.astype(jnp.float32)
    sigmoid_gate = jax.nn.sigmoid(gate_value)
    activated = gate_value * sigmoid_gate
    hidden = sync((activated * up_value).astype(bf16))[0]
    order = jnp.asarray(regroup())

    own_hidden = [hidden[:, a:b] for a, b in CUTS]

    rows = [down_weight] + [shift(down_weight, "y", -step) for step in (1, 2, 3)]
    own_part, other_part = turn(ixl, order, cotangent)
    from_left = shift_x(other_part, 1)
    from_right = shift_x(other_part, -1)
    from_far = shift_x(own_part, 2)
    rows, from_left, from_right, from_far, own_hidden = sync(rows, from_left, from_right, from_far, own_hidden)

    held = jnp.stack(rows + rows[:3])
    held = lax.dynamic_slice_in_dim(held, (4 - iy) % 4, 4, 0)
    weight = lax.all_gather(held, "z", axis=1, tiled=True).reshape(1280, 1792)
    pair_hidden = [shift(h, "xl", 1) for h in own_hidden]
    mine = jnp.stack([own_part, from_far, pick(low, from_right, from_left), pick(low, from_left, from_right)])
    theirs = shift(mine, "c", 1)
    theirs = sync(theirs)[0]

    def whole(same, other):
        here = [pick(core0, mine[same], theirs[same]), pick(core0, theirs[same], mine[same])]
        there = [pick(core0, mine[other], theirs[other]), pick(core0, theirs[other], mine[other])]
        blocks = [pick(first, here[0], there[0]), pick(first, here[1], there[1])]
        blocks += [pick(first, there[0], here[0]), pick(first, there[1], here[1])]
        return jnp.concatenate(blocks, axis=0)

    cot_own, cot_pair = whole(0, 1), whole(2, 3)

    cot_own4, cot_pair4 = cot_own.reshape(4, 320, 320), cot_pair.reshape(4, 320, 320)

    def block(step, q):
        pair = [lax.dynamic_index_in_dim(t, (iy + step) % 4, 0, False) for t in (cot_own4, cot_pair4)]
        return dot(pair[0], own_hidden[q], 1, 0) + dot(pair[1], pair_hidden[q], 1, 0)

    def wide(value):
        return value.astype(jnp.float32)

    up_two = shift(block(2, 0).astype(bf16), "y", 1)
    down_one = shift(block(-1, 0).astype(bf16), "y", -1)
    up_last = shift(block(1, 1).astype(bf16), "y", 1)
    down_two = shift(block(2, 1).astype(bf16), "y", -1)
    up_two, down_one, up_last, down_two = sync(up_two, down_one, up_last, down_two)
    up_one = shift((block(1, 0) + wide(up_two)).astype(bf16), "y", 1)
    down_last = shift((block(-1, 1) + wide(down_two)).astype(bf16), "y", -1)
    summed0 = block(0, 0) + wide(down_one)
    summed1 = block(0, 1) + wide(up_last)

    share = dot(cot_pair, weight, 0, 0, bf16)
    share, weight = sync(share, weight)
    give, keep = output_parts(ic, hidden, pair_hidden, weight)
    up_one, down_last, summed0, summed1, share, give, keep = sync(
        up_one, down_last, summed0, summed1, share, give, keep
    )
    summed = jnp.concatenate([summed0 + wide(up_one), summed1 + wide(down_last)], axis=1).reshape(8, 40, 1792)

    def part(step):
        return lax.dynamic_index_in_dim(summed, (iz + step) % 8, 0, False)

    half = CUTS[0][1]

    def hop(way):
        four = part(4)[:, :half] if way == 1 else part(4)[:, half:]
        return shift(jnp.concatenate([part(3 * way), four], axis=1).astype(bf16), "z", 2 * way)

    far_sums = {way: hop(way) for way in (1, -1)}

    own_share = dot(cot_own, weight, 0, 0)
    far_sums, share, own_share, taken, keep, summed = sync(
        far_sums, shift(share, "xl", 1), own_share, shift(give, "c", 1), keep, summed
    )
    added = [[keep[2 * t + k] + wide(taken[2 * t + k]) for k in range(2)] for t in range(2)]
    near = [pick(first, a[0], a[1]) for a in added]
    far = [pick(first, a[1], a[0]).astype(bf16) for a in added]
    near_pair = near[1].astype(bf16)
    left = shift_x(pick(low, near_pair, far[1]), 1)
    right = shift_x(pick(low, far[1], near_pair), -1)
    across = shift_x(far[0], 2)
    weight_grad = part(0)
    sums = []
    for way in (1, -1):
        got = wide(far_sums[way])
        one = part(way) + got[:, :1792]
        two = part(2 * way)
        if way == 1:
            two = jnp.concatenate([two[:, :half] + got[:, 1792:], two[:, half:]], axis=1)
        else:
            two = jnp.concatenate([two[:, :half], two[:, half:] + got[:, 1792:]], axis=1)
        sums.append(shift(two.astype(bf16), "z", 2 * way))
        sums.append(shift(one.astype(bf16), "z", way))
    left, right, share = sync(left, right, share)
    grad_hidden = own_share + wide(share)
    weight_grad = weight_grad + sum(wide(value) for value in sums)

    grad_gate = (
        grad_hidden * up_value * sigmoid_gate * (1.0 + gate_value * (1.0 - sigmoid_gate))
    ).astype(bf16)
    grad_up = (grad_hidden * activated).astype(bf16)
    own_cols = (near[0] + wide(across)).astype(bf16)
    other_cols = (wide(left) + wide(right)).astype(bf16)
    low_cols, high_cols = pick(low, own_cols, other_cols), pick(low, other_cols, own_cols)
    mixed = (dot(low_cols, order[:320], 1, 0) + dot(high_cols, order[320:], 1, 0)).astype(bf16)
    return (mixed, grad_gate, grad_up, weight_grad)


def solution(mesh):
    fine = Mesh(mesh.devices.reshape(4, 8, 2, 2, 2), ("y", "z", "xl", "xh", "c"))
    placed = P(("y", "z", "xl"), ("xh", "c"))
    return jax.shard_map(
        shards,
        mesh=fine,
        in_specs=(placed,) * 4,
        out_specs=(placed,) * 4,
        check_vma=False,
    )
```

```python
import jax
import jax.numpy as jnp
import numpy as np
from jax import lax
from jax.experimental import pallas as pl
from jax.experimental.pallas import tpu as pltpu
from jax.sharding import Mesh, PartitionSpec as P

SIZES = {"y": 4, "z": 8, "xl": 2, "xh": 2, "c": 2}
CUTS = ((0, 896), (896, 1792))


def shift(value, axis, step):
    n = SIZES[axis]
    return lax.ppermute(value, axis, [(i, (i + step) % n) for i in range(n)])


def shift_x(value, step):
    def place(x):
        return (x % 2) * 2 + x // 2

    return lax.ppermute(value, ("xl", "xh"), [(place(x), place((x + step) % 4)) for x in range(4)])


def regroup():
    order = np.arange(640).reshape(8, 2, 40).transpose(1, 0, 2).reshape(-1)
    return np.eye(640, dtype=np.float32)[order].astype(jnp.bfloat16)


def dot(a, b, ca, cb, kind=jnp.float32):
    return lax.dot_general(a, b, (((ca,), (cb,)), ((), ())), preferred_element_type=jnp.float32).astype(kind)


def pick(flag, a, b):
    return jnp.where(flag, a, b)


def sync(*values):
    return lax.optimization_barrier(values)


def turn_kernel(which, order, cotangent, own, other):
    i = which[0]
    for place, part in ((i, own), (1 - i, other)):
        part[...] = dot(order[place], cotangent[...], 1, 1, part.dtype)


def turn(which, order, cotangent):
    vmem = pl.BlockSpec(memory_space=pltpu.VMEM)
    return pl.pallas_call(
        turn_kernel,
        out_shape=[jax.ShapeDtypeStruct((320, 320), jnp.bfloat16)] * 2,
        in_specs=[pl.BlockSpec(memory_space=pltpu.SMEM), vmem, vmem],
        out_specs=[vmem, vmem],
        cost_estimate=pl.CostEstimate(flops=2 * 640 * 640 * 320, bytes_accessed=1_700_000, transcendentals=0),
    )(which.reshape(1).astype(jnp.int32), order.reshape(2, 320, 640), cotangent)


def output_kernel(which, own, pair0, pair1, weight, give, keep):
    core = which[0]
    for k in range(2):
        for slice_of, out in ((1 - core, give), (core, keep)):
            rows = pl.ds(pl.multiple_of((2 * k + slice_of) * 320, 320), 320)
            out[k] = dot(own[...], weight[rows, :], 1, 1, out.dtype)
            half = CUTS[0][1]
            value = dot(pair0[...], weight[rows, :half], 1, 1) + dot(pair1[...], weight[rows, half:], 1, 1)
            out[2 + k] = value.astype(out.dtype)


def output_parts(which, own, pair, weight):
    vmem = pl.BlockSpec(memory_space=pltpu.VMEM)
    return pl.pallas_call(
        output_kernel,
        out_shape=[jax.ShapeDtypeStruct((4, 320, 320), kind) for kind in (jnp.bfloat16, jnp.float32)],
        in_specs=[pl.BlockSpec(memory_space=pltpu.SMEM), vmem, vmem, vmem, vmem],
        out_specs=[vmem, vmem],
        compiler_params=pltpu.CompilerParams(vmem_limit_bytes=40 * 2**20),
        cost_estimate=pl.CostEstimate(flops=0, bytes_accessed=0, transcendentals=0),
    )(which.reshape(1).astype(jnp.int32), own, *pair, weight)


def shards(gate_pre, up_pre, down_weight, cotangent):
    bf16 = jnp.bfloat16
    iy, iz, ixl, ixh, ic = (lax.axis_index(a) for a in ("y", "z", "xl", "xh", "c"))
    low, first, core0 = ixl == 0, ixh == 0, ic == 0
    gate_value = gate_pre.astype(jnp.float32)
    up_value = up_pre.astype(jnp.float32)
    sigmoid_gate = jax.nn.sigmoid(gate_value)
    activated = gate_value * sigmoid_gate
    hidden = sync((activated * up_value).astype(bf16))[0]
    order = jnp.asarray(regroup())

    own_hidden = [hidden[:, a:b] for a, b in CUTS]

    rows = [down_weight] + [shift(down_weight, "y", -step) for step in (1, 2, 3)]
    own_part, other_part = turn(ixl, order, cotangent)
    from_left = shift_x(other_part, 1)
    from_right = shift_x(other_part, -1)
    from_far = shift_x(own_part, 2)
    rows, from_left, from_right, from_far, own_hidden = sync(rows, from_left, from_right, from_far, own_hidden)

    held = jnp.stack(rows + rows[:3])
    held = lax.dynamic_slice_in_dim(held, (4 - iy) % 4, 4, 0)
    weight = lax.all_gather(held, "z", axis=1, tiled=True).reshape(1280, 1792)
    pair_hidden = [shift(h, "xl", 1) for h in own_hidden]
    mine = jnp.stack([own_part, from_far, pick(low, from_right, from_left), pick(low, from_left, from_right)])
    theirs = shift(mine, "c", 1)
    theirs = sync(theirs)[0]

    def whole(same, other):
        here = [pick(core0, mine[same], theirs[same]), pick(core0, theirs[same], mine[same])]
        there = [pick(core0, mine[other], theirs[other]), pick(core0, theirs[other], mine[other])]
        blocks = [pick(first, here[0], there[0]), pick(first, here[1], there[1])]
        blocks += [pick(first, there[0], here[0]), pick(first, there[1], here[1])]
        return jnp.concatenate(blocks, axis=0)

    cot_own, cot_pair = whole(0, 1), whole(2, 3)

    cot_own4, cot_pair4 = cot_own.reshape(4, 320, 320), cot_pair.reshape(4, 320, 320)

    def block(step, q):
        pair = [lax.dynamic_index_in_dim(t, (iy + step) % 4, 0, False) for t in (cot_own4, cot_pair4)]
        return dot(pair[0], own_hidden[q], 1, 0) + dot(pair[1], pair_hidden[q], 1, 0)

    def wide(value):
        return value.astype(jnp.float32)

    up_two = shift(block(2, 0).astype(bf16), "y", 1)
    down_one = shift(block(-1, 0).astype(bf16), "y", -1)
    up_last = shift(block(1, 1).astype(bf16), "y", 1)
    down_two = shift(block(2, 1).astype(bf16), "y", -1)
    up_two, down_one, up_last, down_two = sync(up_two, down_one, up_last, down_two)
    up_one = shift((block(1, 0) + wide(up_two)).astype(bf16), "y", 1)
    down_last = shift((block(-1, 1) + wide(down_two)).astype(bf16), "y", -1)
    summed0 = block(0, 0) + wide(down_one)
    summed1 = block(0, 1) + wide(up_last)

    share = dot(cot_pair, weight, 0, 0, bf16)
    share, weight = sync(share, weight)
    give, keep = output_parts(ic, hidden, pair_hidden, weight)
    up_one, down_last, summed0, summed1, share, give, keep = sync(
        up_one, down_last, summed0, summed1, share, give, keep
    )
    summed = jnp.concatenate([summed0 + wide(up_one), summed1 + wide(down_last)], axis=1).reshape(8, 40, 1792)

    def part(step):
        return lax.dynamic_index_in_dim(summed, (iz + step) % 8, 0, False)

    half = CUTS[0][1]

    def hop(way):
        four = part(4)[:, :half] if way == 1 else part(4)[:, half:]
        return shift(jnp.concatenate([part(3 * way), four], axis=1).astype(bf16), "z", 2 * way)

    far_sums = {way: hop(way) for way in (1, -1)}

    own_share = dot(cot_own, weight, 0, 0)
    far_sums, share, own_share, taken, keep, summed = sync(
        far_sums, shift(share, "xl", 1), own_share, shift(give, "c", 1), keep, summed
    )
    added = [[keep[2 * t + k] + wide(taken[2 * t + k]) for k in range(2)] for t in range(2)]
    near = [pick(first, a[0], a[1]) for a in added]
    far = [pick(first, a[1], a[0]).astype(bf16) for a in added]
    near_pair = near[1].astype(bf16)
    left = shift_x(pick(low, near_pair, far[1]), 1)
    right = shift_x(pick(low, far[1], near_pair), -1)
    across = shift_x(far[0], 2)
    sums = {}
    for way in (1, -1):
        got = wide(far_sums[way])
        two = part(2 * way)
        if way == 1:
            two = jnp.concatenate([two[:, :half] + got[:, 1792:], two[:, half:]], axis=1)
        else:
            two = jnp.concatenate([two[:, :half], two[:, half:] + got[:, 1792:]], axis=1)
        sums[way] = shift(two.astype(bf16), "z", way)
    for way in (1, -1):
        one = part(way) + wide(far_sums[way])[:, :1792] + wide(sums[way])
        sums[way] = shift(one.astype(bf16), "z", way)
    weight_grad = part(0) + wide(sums[1]) + wide(sums[-1])

    left, right, share = sync(left, right, share)
    grad_hidden = own_share + wide(share)

    grad_gate = (
        grad_hidden * up_value * sigmoid_gate * (1.0 + gate_value * (1.0 - sigmoid_gate))
    ).astype(bf16)
    grad_up = (grad_hidden * activated).astype(bf16)
    own_cols = (near[0] + wide(across)).astype(bf16)
    other_cols = (wide(left) + wide(right)).astype(bf16)
    low_cols, high_cols = pick(low, own_cols, other_cols), pick(low, other_cols, own_cols)
    mixed = (dot(low_cols, order[:320], 1, 0) + dot(high_cols, order[320:], 1, 0)).astype(bf16)
    return (mixed, grad_gate, grad_up, weight_grad)


def solution(mesh):
    fine = Mesh(mesh.devices.reshape(4, 8, 2, 2, 2), ("y", "z", "xl", "xh", "c"))
    placed = P(("y", "z", "xl"), ("xh", "c"))
    return jax.shard_map(
        shards,
        mesh=fine,
        in_specs=(placed,) * 4,
        out_specs=(placed,) * 4,
        check_vma=False,
    )
```

```python
import jax
import jax.numpy as jnp
import numpy as np
from jax import lax
from jax.experimental import pallas as pl
from jax.experimental.pallas import tpu as pltpu
from jax.sharding import Mesh, PartitionSpec as P

SIZES = {"y": 4, "z": 8, "xl": 2, "xh": 2, "c": 2}
CUTS = ((0, 896), (896, 1792))


def shift(value, axis, step):
    n = SIZES[axis]
    return lax.ppermute(value, axis, [(i, (i + step) % n) for i in range(n)])


def shift_x(value, step):
    def place(x):
        return (x % 2) * 2 + x // 2

    return lax.ppermute(value, ("xl", "xh"), [(place(x), place((x + step) % 4)) for x in range(4)])


def regroup():
    order = np.arange(640).reshape(8, 2, 40).transpose(1, 0, 2).reshape(-1)
    return np.eye(640, dtype=np.float32)[order].astype(jnp.bfloat16)


def dot(a, b, ca, cb, kind=jnp.float32):
    return lax.dot_general(a, b, (((ca,), (cb,)), ((), ())), preferred_element_type=jnp.float32).astype(kind)


def pick(flag, a, b):
    return jnp.where(flag, a, b)


def sync(*values):
    return lax.optimization_barrier(values)


def turn_kernel(which, order, cotangent, own, other):
    i = which[0]
    for place, part in ((i, own), (1 - i, other)):
        part[...] = dot(order[place], cotangent[...], 1, 1, part.dtype)


def turn(which, order, cotangent):
    vmem = pl.BlockSpec(memory_space=pltpu.VMEM)
    return pl.pallas_call(
        turn_kernel,
        out_shape=[jax.ShapeDtypeStruct((320, 320), jnp.bfloat16)] * 2,
        in_specs=[pl.BlockSpec(memory_space=pltpu.SMEM), vmem, vmem],
        out_specs=[vmem, vmem],
        cost_estimate=pl.CostEstimate(flops=2 * 640 * 640 * 320, bytes_accessed=1_700_000, transcendentals=0),
    )(which.reshape(1).astype(jnp.int32), order.reshape(2, 320, 640), cotangent)


def output_kernel(which, own, pair0, pair1, weight, give, keep):
    core = which[0]
    for k in range(2):
        for slice_of, out in ((1 - core, give), (core, keep)):
            rows = pl.ds(pl.multiple_of((2 * k + slice_of) * 320, 320), 320)
            out[k] = dot(own[...], weight[rows, :], 1, 1, out.dtype)
            half = CUTS[0][1]
            value = dot(pair0[...], weight[rows, :half], 1, 1) + dot(pair1[...], weight[rows, half:], 1, 1)
            out[2 + k] = value.astype(out.dtype)


def output_parts(which, own, pair, weight):
    vmem = pl.BlockSpec(memory_space=pltpu.VMEM)
    return pl.pallas_call(
        output_kernel,
        out_shape=[jax.ShapeDtypeStruct((4, 320, 320), kind) for kind in (jnp.bfloat16, jnp.float32)],
        in_specs=[pl.BlockSpec(memory_space=pltpu.SMEM), vmem, vmem, vmem, vmem],
        out_specs=[vmem, vmem],
        compiler_params=pltpu.CompilerParams(vmem_limit_bytes=40 * 2**20),
        cost_estimate=pl.CostEstimate(flops=0, bytes_accessed=0, transcendentals=0),
    )(which.reshape(1).astype(jnp.int32), own, *pair, weight)


def shards(gate_pre, up_pre, down_weight, cotangent):
    bf16 = jnp.bfloat16
    iy, iz, ixl, ixh, ic = (lax.axis_index(a) for a in ("y", "z", "xl", "xh", "c"))
    low, first, core0 = ixl == 0, ixh == 0, ic == 0
    gate_value = gate_pre.astype(jnp.float32)
    up_value = up_pre.astype(jnp.float32)
    sigmoid_gate = jax.nn.sigmoid(gate_value)
    activated = gate_value * sigmoid_gate
    hidden = sync((activated * up_value).astype(bf16))[0]
    order = jnp.asarray(regroup())

    own_hidden = [hidden[:, a:b] for a, b in CUTS]

    rows = [down_weight] + [shift(down_weight, "y", -step) for step in (1, 2, 3)]
    own_part, other_part = turn(ixl, order, cotangent)
    from_left = shift_x(other_part, 1)
    from_right = shift_x(other_part, -1)
    from_far = shift_x(own_part, 2)
    rows, from_left, from_right, from_far, own_hidden = sync(rows, from_left, from_right, from_far, own_hidden)

    held = jnp.stack([lax.select_n((place - iy) % 4, *rows) for place in range(4)])
    weight = lax.all_gather(held, "z", axis=1, tiled=True).reshape(1280, 1792)
    pair_hidden = [shift(h, "xl", 1) for h in own_hidden]
    mine = jnp.stack([own_part, from_far, pick(low, from_right, from_left), pick(low, from_left, from_right)])
    theirs = shift(mine, "c", 1)
    theirs = sync(theirs)[0]

    def whole(same, other):
        here = [pick(core0, mine[same], theirs[same]), pick(core0, theirs[same], mine[same])]
        there = [pick(core0, mine[other], theirs[other]), pick(core0, theirs[other], mine[other])]
        blocks = [pick(first, here[0], there[0]), pick(first, here[1], there[1])]
        blocks += [pick(first, there[0], here[0]), pick(first, there[1], here[1])]
        return jnp.concatenate(blocks, axis=0)

    cot_own, cot_pair = whole(0, 1), whole(2, 3)

    cot_own4, cot_pair4 = cot_own.reshape(4, 320, 320), cot_pair.reshape(4, 320, 320)

    def block(step, q):
        pair = [lax.dynamic_index_in_dim(t, (iy + step) % 4, 0, False) for t in (cot_own4, cot_pair4)]
        return dot(pair[0], own_hidden[q], 1, 0) + dot(pair[1], pair_hidden[q], 1, 0)

    def wide(value):
        return value.astype(jnp.float32)

    up_two = shift(block(2, 0).astype(bf16), "y", 1)
    down_one = shift(block(-1, 0).astype(bf16), "y", -1)
    up_last = shift(block(1, 1).astype(bf16), "y", 1)
    down_two = shift(block(2, 1).astype(bf16), "y", -1)
    up_two, down_one, up_last, down_two = sync(up_two, down_one, up_last, down_two)
    up_one = shift((block(1, 0) + wide(up_two)).astype(bf16), "y", 1)
    down_last = shift((block(-1, 1) + wide(down_two)).astype(bf16), "y", -1)
    summed0 = block(0, 0) + wide(down_one)
    summed1 = block(0, 1) + wide(up_last)

    share = dot(cot_pair, weight, 0, 0, bf16)
    share, weight = sync(share, weight)
    give, keep = output_parts(ic, hidden, pair_hidden, weight)
    up_one, down_last, summed0, summed1, share, give, keep = sync(
        up_one, down_last, summed0, summed1, share, give, keep
    )
    summed = jnp.concatenate([summed0 + wide(up_one), summed1 + wide(down_last)], axis=1).reshape(8, 40, 1792)

    def part(step):
        return lax.dynamic_index_in_dim(summed, (iz + step) % 8, 0, False)

    half = CUTS[0][1]

    def hop(way):
        four = part(4)[:, :half] if way == 1 else part(4)[:, half:]
        return shift(jnp.concatenate([part(3 * way), four], axis=1).astype(bf16), "z", 2 * way)

    far_sums = {way: hop(way) for way in (1, -1)}

    own_share = dot(cot_own, weight, 0, 0)
    far_sums, share, own_share, taken, keep, summed = sync(
        far_sums, shift(share, "xl", 1), own_share, shift(give, "c", 1), keep, summed
    )
    added = [[keep[2 * t + k] + wide(taken[2 * t + k]) for k in range(2)] for t in range(2)]
    near = [pick(first, a[0], a[1]) for a in added]
    far = [pick(first, a[1], a[0]).astype(bf16) for a in added]
    near_pair = near[1].astype(bf16)
    left = shift_x(pick(low, near_pair, far[1]), 1)
    right = shift_x(pick(low, far[1], near_pair), -1)
    across = shift_x(far[0], 2)
    sums = {}
    for way in (1, -1):
        got = wide(far_sums[way])
        two = part(2 * way)
        if way == 1:
            two = jnp.concatenate([two[:, :half] + got[:, 1792:], two[:, half:]], axis=1)
        else:
            two = jnp.concatenate([two[:, :half], two[:, half:] + got[:, 1792:]], axis=1)
        sums[way] = shift(two.astype(bf16), "z", way)
    for way in (1, -1):
        one = part(way) + wide(far_sums[way])[:, :1792] + wide(sums[way])
        sums[way] = shift(one.astype(bf16), "z", way)
    weight_grad = part(0) + wide(sums[1]) + wide(sums[-1])

    left, right, share = sync(left, right, share)
    grad_hidden = own_share + wide(share)

    grad_gate = (
        grad_hidden * up_value * sigmoid_gate * (1.0 + gate_value * (1.0 - sigmoid_gate))
    ).astype(bf16)
    grad_up = (grad_hidden * activated).astype(bf16)
    own_cols = (near[0] + wide(across)).astype(bf16)
    other_cols = (wide(left) + wide(right)).astype(bf16)
    low_cols, high_cols = pick(low, own_cols, other_cols), pick(low, other_cols, own_cols)
    mixed = (dot(low_cols, order[:320], 1, 0) + dot(high_cols, order[320:], 1, 0)).astype(bf16)
    return (mixed, grad_gate, grad_up, weight_grad)


def solution(mesh):
    fine = Mesh(mesh.devices.reshape(4, 8, 2, 2, 2), ("y", "z", "xl", "xh", "c"))
    placed = P(("y", "z", "xl"), ("xh", "c"))
    return jax.shard_map(
        shards,
        mesh=fine,
        in_specs=(placed,) * 4,
        out_specs=(placed,) * 4,
        check_vma=False,
    )
```
